32 devices in a mesh: seq: 8 (over z, x), tp: 2 (over core), pd: 2 (over y).
Axes of the slice: x: 2, y: 2, z: 4, core: 2. Of those that a mesh axis runs over, the one named last changes fastest.
Arguments:
- hidden_in: bfloat16 [2, 2048, 2048], P('pd', 'seq'), may hold values from -6 to 6
- input_gain: float32 [2048], replicated, may hold values from 0.5 to 1.5
- w_query: bfloat16 [2048, 2048], P(None, 'tp'), may hold values from -0.125 to 0.125
- w_key: bfloat16 [2048, 256], P(None, 'tp'), may hold values from -0.125 to 0.125
- w_value: bfloat16 [2048, 256], P(None, 'tp'), may hold values from -0.125 to 0.125
- q_gain: float32 [128], replicated, may hold values from 0.1 to 1.9
- k_gain: float32 [128], replicated, may hold values from 0.1 to 1.9
- w_out: bfloat16 [2048, 2048], P('tp'), may hold values from -0.125 to 0.125
- post_gain: float32 [2048], replicated, may hold values from 0.5 to 1.5
- ctx_key: bfloat16 [2, 512, 256], P('pd', 'seq', 'tp'), may hold values from -70 to 70
- ctx_value: bfloat16 [2, 512, 256], P('pd', 'seq', 'tp'), may hold values from -6 to 6
- span_lens: int32 [2, 8], P('pd'), may hold values from 1 to 1024, 2048 in all within a row
- ctx_lens: int32 [2, 8], P('pd'), may hold values from 1 to 256, 512 in all within a row
- route_ids: int32 [2, 2048, 8], P('pd', ('seq', 'tp')), may hold values from 0 to 31, all different within a row; in each aligned block of 128 rows (0 to 127, 128 to 255, ..., all dimensions but the last counted through in order) at most 48 rows name the same one
- route_weights: float32 [2, 2048, 8], P('pd', ('seq', 'tp')), may hold values from 0.05 to 1
- w_gate_up: bfloat16 [32, 2048, 1536], P(('seq', 'tp', 'pd')), may hold values from -0.125 to 0.125
- w_down: bfloat16 [32, 768, 2048], P(('seq', 'tp', 'pd')), may hold values from -0.21875 to 0.21875
- earlier_kv: bfloat16 [8, 2, 2048, 2, 256], P(None, 'pd', 'seq', 'tp'), may hold values from -6 to 6
- page_table: int32 [8, 2, 16, 2], P(None, 'pd', 'seq', 'tp'), may hold values from 0 to 127, as said below
Outputs:
- layer_out: bfloat16 [2, 2048, 2048], P('pd', ('seq', 'tp'))
- decode_cache: bfloat16 [8, 2, 2, 16, 128, 256], P('seq', 'tp', 'pd')
The draws below stay inside these ranges and needn't reach their ends.
Inputs may be any that keep to these rules, and one draw needn't show every extreme that they name: `route_ids`: within the rows of one device no expert is named more than 48 times, a bound that some block reaches. `page_table`: an entry owner * 16 + slot sends the page to that slot of the device at index owner of seq, with the same indices of tp and pd. Every slot of every owner receives exactly one page; one device sends at most 2 pages to one owner, and exactly that many to some owner.
All inputs are finite; a program needn't handle non-finite values.
Results may differ from the reference program's by a relative error of at most 0.015.
Values may be sent and summed in bfloat16 or wider, within the bound.
A program may use at most 128 MiB of HBM per device.

```python
import math
import jax
import jax.numpy as jnp
import numpy as np
from jax import lax

D = 2048
QH = 16
KVH = 2
HD = 128
FF = 768
TOP = 8
REQS = 8
PAGE = 128
LP = 8
TOK_DEV = 256
CTX_DEV = 64
SPAN = 2048
CTX = 512
EXPERTS = 32
CAP = 48
PAGES_DEV = 16
N_SEQ = 8
N_TP = 2
N_PD = 2


def draw_ctx_key(key, part):
    shape = (N_PD, CTX_DEV * N_SEQ, KVH * HD)
    base = jax.random.truncated_normal(key, -6.0, 6.0, shape, jnp.float32)
    return base.astype(jnp.bfloat16)


def table_block(key):
    subkeys = jax.random.split(key, 3)
    source_order = jax.random.permutation(subkeys[0], N_SEQ)
    spread = max(PAGES_DEV, N_SEQ)
    offsets = jax.random.permutation(subkeys[1], spread)[:PAGES_DEV] % N_SEQ
    slot_orders = jax.vmap(lambda subkey: jax.random.permutation(subkey, PAGES_DEV))(jax.random.split(subkeys[2], N_SEQ))
    owners = (source_order[:, None] + offsets[None, :]) % N_SEQ
    slots = slot_orders[owners, jnp.arange(PAGES_DEV)[None, :]]
    values = owners * PAGES_DEV + slots
    per_device = TOK_DEV // PAGE
    values = values.reshape(N_SEQ, LP, per_device).transpose(1, 0, 2).reshape(LP, N_SEQ * per_device)
    return values


def draw_page_table(key, part):
    count = N_PD * KVH
    blocks = jax.vmap(table_block)(jax.random.split(jax.random.fold_in(key, 7), count))
    span_pages = N_SEQ * (TOK_DEV // PAGE)
    return blocks.reshape(N_PD, KVH, LP, span_pages).transpose(2, 0, 3, 1).astype(jnp.int32)


def shard_levels(key, dims, cuts, smallest, high):
    def one(position, parts):
        draws = jax.random.uniform(jax.random.fold_in(jax.random.fold_in(key, 6), position), (parts,), jnp.float32, smallest / len(cuts), high / len(cuts))
        return jnp.repeat(jnp.exp(draws), dims[position] // parts).reshape((-1,) + (1,) * (len(dims) - position - 1))

    factor_of = one(*cuts[0])
    for cut in cuts[1:]:
        factor_of = factor_of * one(*cut)
    return factor_of


def length_profile(count, total, bound, skew):
    loads = [(1 << 20) // math.isqrt(grade ** skew) + 1 for grade in range(2, count + 1)]
    rest, given = total - bound - (count - 1), [1] * (count - 1)
    while rest > 0:
        movable = [i for i in range(count - 1) if given[i] < bound]
        mass, remaining = sum([loads[i] for i in movable]), rest
        for i in movable:
            more = min(bound - given[i], max(1, remaining * loads[i] // mass), rest)
            given[i] = given[i] + more
            rest = rest - more
    return np.array([bound] + given)


def ragged_sizes(own_key, count, total, reach, lean):
    if count == 2:
        one = jax.random.randint(own_key, (), max(1, total - reach), min(reach, total - 1) + 1)
        return jnp.stack([one, total - one])
    tallies = jnp.asarray(length_profile(count, total, reach, lean), jnp.int32)
    couples = (count - 1) // 2
    donor, sink = tallies[1:1 + 2 * couples:2], tallies[2:2 + 2 * couples:2]
    slack = jnp.minimum(donor - 1, reach - sink)
    moved = jax.random.randint(jax.random.fold_in(own_key, 1), (couples,), 0, 1 << 20) % (slack + 1)
    tallies = tallies.at[1:1 + 2 * couples:2].set(donor - moved).at[2:2 + 2 * couples:2].set(sink + moved)
    return tallies[jax.random.permutation(jax.random.fold_in(own_key, 2), count)]


def routed_block(stream_key, own, number, rows, count, top, reach, skew):
    order = jax.random.permutation(stream_key, count)
    packed, common = portions_of(count, rows * top, reach, skew, True), portions_of(count, rows * top, reach, skew, False)
    places = jnp.arange(count)

    def named(sizes, turn):
        used = int((sizes > 0).sum())
        fixed = max(1, used // 4)
        moved = fixed + (places - fixed + turn * (used - fixed)) % max(1, count - fixed)
        return jnp.zeros((count,), jnp.int32).at[order[jnp.where(places < fixed, places, moved)]].set(jnp.asarray(sizes, jnp.int32))

    sizes = jnp.where(number % 4 == 0, named(packed, number // 4), named(common, number - number // 4 - 1))
    mixed = jax.random.permutation(jax.random.fold_in(own, 3), count)
    donor, sink = mixed[0:count // 2 * 2:2], mixed[1:count // 2 * 2:2]
    room = jnp.minimum(sizes[donor] - 1, reach - sizes[sink]) // 2
    room = jnp.where((donor == order[0]) | (sink == order[0]) | (sizes[sink] == 0), 0, jnp.maximum(room, 0))
    moved = jax.random.randint(jax.random.fold_in(own, 4), (count // 2,), 0, 1 << 20) % (room + 1)
    sizes = sizes.at[donor].add(-moved).at[sink].add(moved)
    labels = jnp.searchsorted(jnp.cumsum(sizes), jnp.arange(rows * top), side="right").astype(jnp.int32)
    grid = labels.reshape(top, rows).T
    grid = grid[jax.random.permutation(jax.random.fold_in(own, 1), rows)]
    turn = jax.random.randint(jax.random.fold_in(own, 2), (rows, 1), 0, top)
    return jnp.take_along_axis(grid, (jnp.arange(top)[None, :] + turn) % top, axis=1)


def portions_of(count, total, most, slope, full):
    portions = [(1 << 20) // math.isqrt(grade ** slope) + 1 for grade in range(1, count + 1)]
    largest = most if full else min(most, max(-(-total // count), total * portions[0] // sum(portions)))
    least = 1 if total - largest >= count - 1 else 0
    given, rest = [largest] + [least] * (count - 1), total - largest - least * (count - 1)
    while rest > 0:
        movable = [i for i in range(1, count) if given[i] < largest] or [i for i in range(1, count) if given[i] < most]
        pool, budget = sum([portions[i] for i in movable]), rest
        for i in movable:
            more = min(most - given[i], max(1, budget * portions[i] // pool), rest)
            given[i] = given[i] + more
            rest = rest - more
    return np.array(given)


def gaussian(own_key, dims, scale, reach, cuts=(), held_as=jnp.bfloat16):
    loudness = shard_levels(own_key, dims, cuts, -0.22, 0.18) if cuts else 1.0
    values = jax.random.normal(own_key, dims, jnp.float32) * scale * loudness
    return jnp.minimum(jnp.maximum(values, -reach), reach).astype(held_as)


def setup_inputs(seed: int = 0) -> dict:
    key_list = jax.random.split(jax.random.key(seed), 20)
    hidden_in = gaussian(key_list[0], (N_PD, SPAN, D), 1.0, 6.0, ((0, 2), (1, 8)))
    input_gain = jnp.clip(1.0 + 0.1 * jax.random.normal(key_list[1], (D,), jnp.float32), 0.5, 1.5)
    w_query = gaussian(key_list[2], (D, QH * HD), D ** -0.5, 0.125, ((1, 2),))
    w_key = gaussian(key_list[3], (D, KVH * HD), D ** -0.5, 0.125, ((1, 2),))
    w_value = gaussian(key_list[4], (D, KVH * HD), D ** -0.5, 0.125, ((1, 2),))
    q_gain = jnp.clip(1.0 + 0.18 * jax.random.normal(key_list[5], (HD,), jnp.float32), 0.1, 1.9)
    k_gain = jnp.clip(1.0 + 0.18 * jax.random.normal(key_list[6], (HD,), jnp.float32), 0.1, 1.9)
    w_out = gaussian(key_list[7], (QH * HD, D), (QH * HD) ** -0.5, 0.125, ((0, 2),))
    post_gain = jnp.clip(1.0 + 0.1 * jax.random.normal(key_list[8], (D,), jnp.float32), 0.5, 1.5)
    ctx_key = draw_ctx_key(jax.random.fold_in(key_list[19], 71), 0)
    ctx_value = gaussian(key_list[10], (N_PD, CTX, KVH * HD), 1.0, 6.0, ((0, 2), (1, 8), (2, 2)))
    span_lens = jax.vmap(lambda own: ragged_sizes(own, REQS, TOK_DEV * N_SEQ, TOK_DEV * N_SEQ // 2, 2))(jax.random.split(key_list[11], N_PD)).reshape((N_PD, REQS)).astype(jnp.int32)
    ctx_lens = jax.vmap(lambda own: ragged_sizes(own, REQS, CTX_DEV * N_SEQ, CTX_DEV * N_SEQ // 2, 2))(jax.random.split(key_list[12], N_PD)).reshape((N_PD, REQS)).astype(jnp.int32)
    route_ids_keys = jax.random.split(jax.random.fold_in(key_list[13], 1), N_PD * SPAN // (TOK_DEV // N_TP))
    route_ids_turns = jax.random.permutation(jax.random.fold_in(key_list[13], 3), N_PD * SPAN // (TOK_DEV // N_TP))
    route_ids = jax.vmap(lambda own, number: routed_block(jax.random.fold_in(key_list[13], 2), own, number, TOK_DEV // N_TP, EXPERTS, TOP, CAP, 2))(route_ids_keys, route_ids_turns).reshape((N_PD, SPAN, TOP))
    route_weights = jnp.clip(jnp.exp(math.log(1.0) - 2.9957323 * jax.random.uniform(key_list[14], (N_PD, SPAN, TOP), jnp.float32) ** shard_levels(key_list[14], (N_PD, SPAN, TOP), ((0, 2), (1, 16)), -0.2, 0.2)), 0.05, 1.0)
    w_gate_up = gaussian(key_list[15], (EXPERTS, D, 2 * FF), D ** -0.5, 0.125, ((0, 32),))
    w_down = gaussian(key_list[16], (EXPERTS, FF, D), FF ** -0.5, 0.21875, ((0, 32),))
    earlier_kv = gaussian(key_list[17], (LP, N_PD, SPAN, KVH, 2 * HD), 1.0, 6.0, ((1, 2), (2, 8), (3, 2)))
    page_table = draw_page_table(jax.random.fold_in(key_list[19], 71), 0)
    return {"hidden_in": hidden_in, "input_gain": input_gain, "w_query": w_query, "w_key": w_key, "w_value": w_value, "q_gain": q_gain, "k_gain": k_gain, "w_out": w_out, "post_gain": post_gain, "ctx_key": ctx_key, "ctx_value": ctx_value, "span_lens": span_lens, "ctx_lens": ctx_lens, "route_ids": route_ids, "route_weights": route_weights, "w_gate_up": w_gate_up, "w_down": w_down, "earlier_kv": earlier_kv, "page_table": page_table}


def rms_norm(values, gain):
    return values * lax.rsqrt(lax.optimization_barrier(jnp.mean(values * values, axis=-1, keepdims=True)) + 1e-06) * gain

def rotate(values, places):
    half = values.shape[-1] // 2
    freq = jnp.exp(jnp.arange(half, dtype=jnp.float32) * (-2.0 * math.log(1000000.0) / values.shape[-1]))
    angle = places.astype(jnp.float32)[:, None] * freq[None, :]
    cosine = jnp.cos(angle)[:, None, :]
    sine = jnp.sin(angle)[:, None, :]
    first = values[..., :half]
    second = values[..., half:]
    return jnp.concatenate([first * cosine - second * sine, second * cosine + first * sine], axis=-1)

def query_places(lengths, context_lengths, places):
    ends = jnp.cumsum(lengths).astype(jnp.int32)
    starts = ends - lengths
    request = lax.optimization_barrier(jnp.sum((places[:, None] >= ends[None, :]).astype(jnp.int32), axis=1)).astype(jnp.int32)
    member = request[:, None] == jnp.arange(lengths.shape[0], dtype=jnp.int32)[None, :]
    first = lax.optimization_barrier(jnp.sum(jnp.where(member, starts[None, :], 0), axis=1)).astype(jnp.int32)
    prior = lax.optimization_barrier(jnp.sum(jnp.where(member, context_lengths[None, :], 0), axis=1)).astype(jnp.int32)
    return (request, (places - first + prior).astype(jnp.int32))

def context_places(context_lengths, places):
    ends = jnp.cumsum(context_lengths).astype(jnp.int32)
    starts = ends - context_lengths
    request = lax.optimization_barrier(jnp.sum((places[:, None] >= ends[None, :]).astype(jnp.int32), axis=1)).astype(jnp.int32)
    member = request[:, None] == jnp.arange(context_lengths.shape[0], dtype=jnp.int32)[None, :]
    first = lax.optimization_barrier(jnp.sum(jnp.where(member, starts[None, :], 0), axis=1)).astype(jnp.int32)
    return (request, (places - first).astype(jnp.int32))

def group_attention(tokens, input_gain, w_query, w_key, w_value, q_gain, k_gain, w_out, post_gain, context_keys, context_values, lengths, context_lengths):
    span_places = jnp.arange(SPAN, dtype=jnp.int32)
    query_req, query_pos = query_places(lengths, context_lengths, span_places)
    ctx_req, ctx_pos = context_places(context_lengths, jnp.arange(CTX, dtype=jnp.int32))
    normed = rms_norm(tokens.astype(jnp.float32), input_gain).astype(jnp.bfloat16)
    query = jnp.dot(normed, w_query, preferred_element_type=jnp.float32).reshape(SPAN, QH, HD)
    key_proj = jnp.dot(normed, w_key, preferred_element_type=jnp.float32).reshape(SPAN, KVH, HD)
    value_proj = jnp.dot(normed, w_value, preferred_element_type=jnp.float32).astype(jnp.bfloat16)
    queries = rotate(rms_norm(query, q_gain), query_pos).astype(jnp.bfloat16)
    span_keys = rotate(rms_norm(key_proj, k_gain), query_pos).astype(jnp.bfloat16)
    all_keys = jnp.concatenate([context_keys.reshape(CTX, KVH, HD), span_keys], axis=0).astype(jnp.float32)
    all_values = jnp.concatenate([context_values.reshape(CTX, KVH, HD), value_proj.reshape(SPAN, KVH, HD)], axis=0).astype(jnp.float32)
    key_req = jnp.concatenate([ctx_req, query_req], axis=0)
    key_pos = jnp.concatenate([ctx_pos, query_pos], axis=0)
    group = QH // KVH
    block_rows = math.gcd(512, SPAN)
    count = SPAN // block_rows
    scale = 1.0 / math.sqrt(HD)

    def attend(items):
        query_block, req_block, pos_block = items
        scores = jnp.einsum('qhgd,khd->hgqk', query_block.astype(jnp.float32), all_keys) * scale
        visible = (req_block[:, None] == key_req[None, :]) & (key_pos[None, :] <= pos_block[:, None])
        scores = jnp.where(visible[None, None], scores, -jnp.inf)
        largest = lax.optimization_barrier(jnp.max(scores, axis=-1, keepdims=True))
        expo = jnp.exp(scores - largest)
        total = lax.optimization_barrier(jnp.sum(expo, axis=-1))
        probs = lax.optimization_barrier(expo.astype(jnp.bfloat16)).astype(jnp.float32)
        numer = jnp.einsum('hgqk,khd->hgqd', probs, all_values)
        result = numer / total[..., None]
        return result.transpose(2, 0, 1, 3).reshape(block_rows, QH * HD).astype(jnp.bfloat16)
    attn = lax.map(attend, (queries.reshape(count, block_rows, KVH, group, HD), query_req.reshape(count, block_rows), query_pos.reshape(count, block_rows)))
    attn = attn.reshape(SPAN, QH * HD)
    proj = jnp.dot(attn, w_out, preferred_element_type=jnp.float32)
    resid = (tokens.astype(jnp.float32) + proj).astype(jnp.bfloat16)
    mixed = rms_norm(resid.astype(jnp.float32), post_gain).astype(jnp.bfloat16)
    return (resid, mixed)

def reference(hidden_in, input_gain, w_query, w_key, w_value, q_gain, k_gain, w_out, post_gain, ctx_key, ctx_value, span_lens, ctx_lens, route_ids, route_weights, w_gate_up, w_down, earlier_kv, page_table):
    resid_parts = []
    mixed_parts = []
    for group_index in range(N_PD):
        resid, mixed = group_attention(hidden_in[group_index], input_gain, w_query, w_key, w_value, q_gain, k_gain, w_out, post_gain, ctx_key[group_index], ctx_value[group_index], span_lens[group_index], ctx_lens[group_index])
        resid_parts.append(resid)
        mixed_parts.append(mixed)
    resid_all = jnp.concatenate(resid_parts, axis=0)
    mixed_all = jnp.concatenate(mixed_parts, axis=0)
    row_ids = route_ids.reshape(-1).astype(jnp.int32)
    row_total = row_ids.shape[0]
    row_token = (jnp.arange(row_total, dtype=jnp.int32) // TOP).astype(jnp.int32)
    order = jnp.argsort(row_ids, stable=True).astype(jnp.int32)
    counts = lax.optimization_barrier(jnp.sum((row_ids[:, None] == jnp.arange(EXPERTS, dtype=jnp.int32)[None, :]).astype(jnp.int32), axis=0)).astype(jnp.int32)
    starts = (jnp.cumsum(counts) - counts).astype(jnp.int32)
    most_rows = N_SEQ * N_TP * N_PD * CAP
    padded = jnp.concatenate([order, jnp.zeros((most_rows,), jnp.int32)], axis=0)

    def expert(index):
        picked = lax.dynamic_slice(padded, (starts[index].astype(jnp.int32),), (most_rows,))
        rows = mixed_all[row_token[picked]]
        live = jnp.arange(most_rows, dtype=jnp.int32) < counts[index]
        hidden = jnp.dot(rows, w_gate_up[index], preferred_element_type=jnp.float32)
        act = (jax.nn.silu(hidden[:, :FF]) * hidden[:, FF:]).astype(jnp.bfloat16)
        out_rows = jnp.dot(act, w_down[index], preferred_element_type=jnp.float32).astype(jnp.bfloat16)
        return jnp.where(live[:, None], out_rows, jnp.zeros_like(out_rows))
    expert_rows = lax.map(expert, jnp.arange(EXPERTS, dtype=jnp.int32))
    inverse = jnp.zeros((row_total,), jnp.int32).at[order].set(jnp.arange(row_total, dtype=jnp.int32))
    within = (inverse - starts[row_ids]).astype(jnp.int32)
    gathered = expert_rows[row_ids, within]
    weights = route_weights.reshape(N_PD * SPAN, TOP)
    weights = weights / lax.optimization_barrier(jnp.sum(weights, axis=-1, keepdims=True))
    moe = jnp.einsum('tkd,tk->td', gathered.reshape(N_PD * SPAN, TOP, D).astype(jnp.float32), weights)
    layer_out = (resid_all.astype(jnp.float32) + moe).astype(jnp.bfloat16).reshape(N_PD, SPAN, D)
    span_pages = SPAN // PAGE
    pages = earlier_kv.reshape(LP, N_PD, span_pages, PAGE, KVH, 2 * HD).transpose(0, 1, 2, 4, 3, 5)
    owners = (page_table // PAGES_DEV).astype(jnp.int32)
    slots = (page_table % PAGES_DEV).astype(jnp.int32)
    group_index_all = lax.broadcasted_iota(jnp.int32, page_table.shape, 1)
    head_index_all = lax.broadcasted_iota(jnp.int32, page_table.shape, 3)
    decode_cache = jnp.zeros((N_SEQ, KVH, N_PD, PAGES_DEV, PAGE, 2 * HD), jnp.bfloat16)
    decode_cache = decode_cache.at[owners, head_index_all, group_index_all, slots].set(pages)
    return (layer_out, decode_cache)
```

```python
import functools
import math

import jax
import jax.numpy as jnp
from jax import lax
from jax.experimental import pallas as pl
from jax.experimental.pallas import tpu as pltpu
from jax.sharding import PartitionSpec as P

PAGE = 128
MESH = pl.DeviceIdType.MESH
DEPTH = 4


def remote(src, dst, send, recv, device):
    return pltpu.make_async_remote_copy(
        src_ref=src,
        dst_ref=dst,
        send_sem=send,
        recv_sem=recv,
        device_id=device,
        device_id_type=MESH,
    )


def position():
    seq = lax.axis_index("seq")
    return seq, seq // 2, seq % 2, lax.axis_index("pd"), lax.axis_index("tp")


def greet(full):
    seq, mz, mx, my, mc = position()
    barrier = pltpu.get_barrier_semaphore()

    @pl.when(mz > 0)
    def _():
        pl.semaphore_signal(barrier, inc=1, device_id={"seq": seq - 2}, device_id_type=MESH)

    @pl.when(mz < DEPTH - 1)
    def _():
        pl.semaphore_signal(barrier, inc=1, device_id={"seq": seq + 2}, device_id_type=MESH)

    others = [{"seq": mz * 2 + 1 - mx}]
    if full:
        others += [{"pd": 1 - my}, {"tp": 1 - mc}]
    for other in others:
        pl.semaphore_signal(barrier, inc=1, device_id=other, device_id_type=MESH)
    ends = (mz > 0).astype(jnp.int32) + (mz < DEPTH - 1).astype(jnp.int32)
    pl.semaphore_wait(barrier, len(others) + ends)


def gather_kernel(full, in_ref, out_ref, lsem, zu, zd, zr, xs, xr, ys, yr, es, er, fs, fr, cs, cr):
    seq, mz, mx, my, mc = position()
    half = in_ref.shape[0] // 2
    xdev, ydev, cdev = {"seq": mz * 2 + 1 - mx}, {"pd": 1 - my}, {"tp": 1 - mc}

    def slot(o, x, y):
        return out_ref.at[o, x, y, mc] if full else out_ref.at[o, x]

    def core_slot(o, x, y, c):
        return out_ref.at[o, x, y, c]

    first, second = pl.ds(0, half), pl.ds(half, half)
    own = pltpu.make_async_copy(in_ref, slot(mz, mx, my), lsem)

    def zup(src, o):
        return remote(src, slot(o, mx, my), zu.at[o], zr.at[o], {"seq": seq + 2})

    def zdown(src, o):
        return remote(src, slot(o, mx, my), zd.at[o], zr.at[o], {"seq": seq - 2})

    def xcopy(src, o, x):
        return remote(src, slot(o, x, my), xs.at[o], xr.at[o], xdev)

    def ycopy(src, o, y):
        return remote(src, slot(o, mx, y), ys.at[o], yr.at[o], ydev)

    def ecopy(o, x, y):
        part = slot(o, x, y).at[first]
        return remote(part, part, es.at[o], er.at[o], ydev)

    def fcopy(o, x, y):
        part = slot(o, x, y).at[second]
        return remote(part, part, fs.at[o], fr.at[o], xdev)

    def ccopy(src, o, x, y, c):
        k = o * 4 + x * 2 + y
        return remote(src, core_slot(o, x, y, c), cs.at[k], cr.at[k], cdev)

    def have_z(o, src, up, down):
        if up:

            @pl.when(mz < DEPTH - 1)
            def _():
                zup(src, o).start()

        if down:

            @pl.when(mz > 0)
            def _():
                zdown(src, o).start()

        xcopy(src, o, mx).start()
        if full:
            ycopy(src, o, my).start()
            ccopy(src, o, mx, my, mc).start()

    def have_xy(o):
        xcopy(slot(o, 1 - mx, my), o, 1 - mx).wait_recv()
        if full:
            ecopy(o, 1 - mx, my).start()
            ccopy(slot(o, 1 - mx, my), o, 1 - mx, my, mc).start()
            ycopy(slot(o, mx, 1 - my), o, 1 - my).wait_recv()
            fcopy(o, mx, 1 - my).start()
            ccopy(slot(o, mx, 1 - my), o, mx, 1 - my, mc).start()

    def have_diagonal(o):
        if full:
            ecopy(o, 1 - mx, 1 - my).wait_recv()
            fcopy(o, 1 - mx, 1 - my).wait_recv()
            ccopy(slot(o, 1 - mx, 1 - my), o, 1 - mx, 1 - my, mc).start()

    def each(step, action):
        if step == 0:
            action(mz)
        elif step > 0:
            pl.when(mz - step >= 0)(lambda: action(mz - step))
            pl.when(mz + step < DEPTH)(lambda: action(mz + step))

    greet(full)
    have_z(mz, in_ref, True, True)
    own.start()
    for step in range(1, DEPTH):

        @pl.when(mz - step >= 0)
        def _():
            o = mz - step
            zup(slot(o, mx, my), o).wait_recv()
            have_z(o, slot(o, mx, my), True, False)

        @pl.when(mz + step < DEPTH)
        def _():
            o = mz + step
            zup(slot(o, mx, my), o).wait_recv()
            have_z(o, slot(o, mx, my), False, True)

        each(step - 1, have_xy)
        each(step - 2, have_diagonal)
    each(DEPTH - 1, have_xy)
    each(DEPTH - 2, have_diagonal)
    each(DEPTH - 1, have_diagonal)
    for o in range(DEPTH):
        block = slot(o, mx, my)
        pl.when((mz < DEPTH - 1) & (mz >= o))(lambda: zup(block, o).wait_send())
        pl.when((mz > 0) & (mz <= o))(lambda: zdown(block, o).wait_send())
        xcopy(block, o, mx).wait_send()
        if full:
            ycopy(block, o, my).wait_send()
            ecopy(o, 1 - mx, my).wait_send()
            fcopy(o, mx, 1 - my).wait_send()
            for x in range(2):
                for y in range(2):
                    done = ccopy(slot(o, x, y), o, x, y, 1 - mc)
                    done.wait_recv()
                    done.wait_send()
    own.wait()


def gather(block, full, collective_id):
    shape = (DEPTH, 2, 2, 2) if full else (DEPTH, 2)
    dma = pltpu.SemaphoreType.DMA
    return pl.pallas_call(
        functools.partial(gather_kernel, full),
        out_shape=jax.ShapeDtypeStruct(shape + block.shape, block.dtype),
        in_specs=[pl.BlockSpec(memory_space=pl.ANY)],
        out_specs=pl.BlockSpec(memory_space=pl.ANY),
        scratch_shapes=[dma] + [dma((DEPTH,))] * 11 + [dma((4 * DEPTH,))] * 2,
        compiler_params=pltpu.CompilerParams(collective_id=collective_id, has_side_effects=True),
        name="gather_full" if full else "gather_seq",
    )(block)


def combine_kernel(
    part_ref, resid_ref, out_ref, s, cb, dx, dy, xb, yb, zub, zdb,
    ls, cs, cr, dxs, dxr, dys, dyr, xs, xr, ys, yr, zs, zur, zdr,
):
    seq, mz, mx, my, mc = position()
    rows = resid_ref.shape[0]
    half = rows // 2
    xdev, ydev, cdev = {"seq": mz * 2 + 1 - mx}, {"pd": 1 - my}, {"tp": 1 - mc}
    first, second = pl.ds(0, half), pl.ds(half, half)
    step_rows = 16
    lower = mz < 2
    far = jnp.where(lower, 3, 0)
    order = [
        far,
        jnp.where(mz == 0, 2, jnp.where(mz == 1, 0, jnp.where(mz == 2, 3, 1))),
        jnp.where((mz == 0) | (mz == 2), 1, 2),
        mz,
    ]
    middle = (mz == 1) | (mz == 2)

    def load(o, x, y):
        return pltpu.make_async_copy(
            part_ref.at[o, x, y, mc], s.at[o, x, y], ls.at[o * 4 + x * 2 + y]
        )

    def core(o, x, y):
        k = o * 4 + x * 2 + y
        return remote(part_ref.at[o, x, y, 1 - mc], cb.at[o, x, y], cs.at[k], cr.at[k], cdev)

    def diag_x(o):
        return remote(s.at[o, 1 - mx, 1 - my].at[first], dx.at[o], dxs.at[o], dxr.at[o], xdev)

    def diag_y(o):
        return remote(s.at[o, 1 - mx, 1 - my].at[second], dy.at[o], dys.at[o], dyr.at[o], ydev)

    def send_x(o):
        return remote(s.at[o, 1 - mx, my], xb.at[o], xs.at[o], xr.at[o], xdev)

    def send_y(o):
        return remote(s.at[o, mx, 1 - my], yb.at[o], ys.at[o], yr.at[o], ydev)

    def send_up(o):
        return remote(s.at[o, mx, my], zub.at[o], zs.at[o], zur.at[o], {"seq": seq + 2})

    def send_down(o):
        return remote(s.at[o, mx, my], zdb.at[o], zs.at[o], zdr.at[o], {"seq": seq - 2})

    def add(target, start, count, *others):
        @pl.loop(0, count // step_rows)
        def _(i):
            at = pl.ds(pl.multiple_of(start + i * step_rows, step_rows), step_rows)
            total = target[at, :].astype(jnp.float32)
            for other in others:
                there = pl.ds(pl.multiple_of(i * step_rows, step_rows), step_rows)
                total = total + other[there, :].astype(jnp.float32)
            target[at, :] = total.astype(target.dtype)

    def begin(o):
        for x, y in ((1 - mx, 1 - my), (1 - mx, my), (mx, 1 - my), (mx, my)):
            core(o, x, y).start()
            load(o, x, y).start()

    def stage_a(o):
        for x, y in ((1 - mx, 1 - my), (1 - mx, my), (mx, 1 - my), (mx, my)):
            load(o, x, y).wait()
            core(o, x, y).wait_recv()
            add(s.at[o, x, y], 0, rows, cb.at[o, x, y])
            if x is not mx and y is not my:
                diag_x(o).start()
                diag_y(o).start()

    def stage_b(o):
        diag_x(o).wait_recv()
        add(s.at[o, mx, 1 - my], 0, half, dx.at[o])
        send_y(o).start()
        diag_y(o).wait_recv()
        add(s.at[o, 1 - mx, my], half, half, dy.at[o])
        send_x(o).start()

    def pass_on(o, incoming):
        up = o > mz

        @pl.when(up)
        def _():
            if incoming:
                send_up(o).wait_recv()
                add(s.at[o, mx, my], 0, rows, zub.at[o])
            send_up(o).start()

        @pl.when(jnp.logical_not(up))
        def _():
            if incoming:
                send_down(o).wait_recv()
                add(s.at[o, mx, my], 0, rows, zdb.at[o])
            send_down(o).start()

    def stage_c(j):
        o = order[j]
        send_x(o).wait_recv()
        send_y(o).wait_recv()
        add(s.at[o, mx, my], 0, rows, xb.at[o], yb.at[o])
        if j < DEPTH - 1:
            pl.when(jnp.logical_not(middle))(lambda: pass_on(o, False))
        for late in {0: (), 1: (0,), 2: (1, 2), 3: ()}[j]:
            pl.when(middle)(lambda: pass_on(order[late], True))

    greet(True)
    for o in order:
        begin(o)
    for t in range(DEPTH + 2):
        if t < DEPTH:
            stage_a(order[t])
        if 1 <= t <= DEPTH:
            stage_b(order[t - 1])
        if t >= 2:
            stage_c(t - 2)

    pl.when(mz > 0)(lambda: send_up(mz).wait_recv())
    pl.when(mz < DEPTH - 1)(lambda: send_down(mz).wait_recv())

    @pl.loop(0, rows // step_rows)
    def _(i):
        at = pl.ds(pl.multiple_of(i * step_rows, step_rows), step_rows)
        out_ref[at, :] = s[mz, mx, my, at, :].astype(jnp.float32) + resid_ref[at, :].astype(
            jnp.float32
        )

    @pl.when(mz > 0)
    def _():
        add(out_ref, 0, rows, zub.at[mz])

    @pl.when(mz < DEPTH - 1)
    def _():
        add(out_ref, 0, rows, zdb.at[mz])

    for o in range(DEPTH):
        for x in range(2):
            for y in range(2):
                core(o, x, y).wait_send()
        diag_x(o).wait_send()
        diag_y(o).wait_send()
        send_x(o).wait_send()
        send_y(o).wait_send()
        pl.when(mz != o)(lambda: send_up(o).wait_send())


def combine(partial, resid, collective_id):
    rows, width = resid.shape
    dma = pltpu.SemaphoreType.DMA
    bf16 = jnp.bfloat16
    vmem = pl.BlockSpec(memory_space=pltpu.VMEM)
    return pl.pallas_call(
        combine_kernel,
        out_shape=jax.ShapeDtypeStruct((rows, width), jnp.float32),
        in_specs=[pl.BlockSpec(memory_space=pl.ANY), vmem],
        out_specs=vmem,
        scratch_shapes=[
            pltpu.VMEM((DEPTH, 2, 2, rows, width), bf16),
            pltpu.VMEM((DEPTH, 2, 2, rows, width), bf16),
            pltpu.VMEM((DEPTH, rows // 2, width), bf16),
            pltpu.VMEM((DEPTH, rows // 2, width), bf16),
        ]
        + [pltpu.VMEM((DEPTH, rows, width), bf16)] * 4
        + [dma((4 * DEPTH,))] * 3
        + [dma((DEPTH,))] * 11,
        compiler_params=pltpu.CompilerParams(
            collective_id=collective_id, has_side_effects=True, vmem_limit_bytes=48 << 20
        ),
        name="combine",
    )(partial, resid)


def rms_norm(values, gain):
    return values * lax.rsqrt(jnp.mean(values * values, axis=-1, keepdims=True) + 1e-06) * gain


def rotate(values, places):
    half = values.shape[-1] // 2
    freq = jnp.exp(
        jnp.arange(half, dtype=jnp.float32) * (-2.0 * math.log(1000000.0) / values.shape[-1])
    )
    angle = places.astype(jnp.float32)[:, None] * freq[None, :]
    cosine = jnp.cos(angle)[:, None, :]
    sine = jnp.sin(angle)[:, None, :]
    first = values[..., :half]
    second = values[..., half:]
    return jnp.concatenate(
        [first * cosine - second * sine, second * cosine + first * sine], axis=-1
    )


def query_places(lengths, context_lengths, places):
    ends = jnp.cumsum(lengths)
    starts = ends - lengths
    request = jnp.sum((places[:, None] >= ends[None, :]).astype(jnp.int32), axis=1)
    member = request[:, None] == jnp.arange(lengths.shape[0], dtype=jnp.int32)[None, :]
    first = jnp.sum(jnp.where(member, starts[None, :], 0), axis=1)
    prior = jnp.sum(jnp.where(member, context_lengths[None, :], 0), axis=1)
    return (request, places - first + prior)


def context_places(context_lengths, places):
    ends = jnp.cumsum(context_lengths)
    starts = ends - context_lengths
    request = jnp.sum((places[:, None] >= ends[None, :]).astype(jnp.int32), axis=1)
    member = request[:, None] == jnp.arange(context_lengths.shape[0], dtype=jnp.int32)[None, :]
    first = jnp.sum(jnp.where(member, starts[None, :], 0), axis=1)
    return (request, places - first)


def expert_mlp(arrived, w_gate_up, w_down):
    hidden = jnp.einsum("sejd,edf->sejf", arrived, w_gate_up, preferred_element_type=jnp.float32)
    inner = hidden.shape[-1] // 2
    act = (jax.nn.silu(hidden[..., :inner]) * hidden[..., inner:]).astype(jnp.bfloat16)
    return jnp.einsum("sejf,efd->sejd", act, w_down, preferred_element_type=jnp.float32).astype(
        jnp.bfloat16
    )


def shards(
    hidden_in,
    input_gain,
    w_query,
    w_key,
    w_value,
    q_gain,
    k_gain,
    w_out,
    post_gain,
    ctx_key,
    ctx_value,
    span_lens,
    ctx_lens,
    route_ids,
    route_weights,
    w_gate_up,
    w_down,
    earlier_kv,
    page_table,
):
    tokens = hidden_in[0]
    tok_count = tokens.shape[0]
    width = tokens.shape[1]
    ctx_count = ctx_key.shape[1]
    head_dim = q_gain.shape[0]
    seq_index = lax.axis_index("seq")
    span_places = seq_index * tok_count + jnp.arange(tok_count, dtype=jnp.int32)
    ctx_index = seq_index * ctx_count + jnp.arange(ctx_count, dtype=jnp.int32)
    query_req, query_pos = query_places(span_lens[0], ctx_lens[0], span_places)
    ctx_req, ctx_pos = context_places(ctx_lens[0], ctx_index)
    normed = rms_norm(tokens.astype(jnp.float32), input_gain).astype(jnp.bfloat16)
    query = jnp.dot(normed, w_query, preferred_element_type=jnp.float32)
    key_proj = jnp.dot(normed, w_key, preferred_element_type=jnp.float32)
    value_proj = jnp.dot(normed, w_value, preferred_element_type=jnp.float32).astype(jnp.bfloat16)
    query_heads = w_query.shape[1] // head_dim
    kv_local = w_key.shape[1] // head_dim
    group = query_heads // kv_local
    queries = rotate(
        rms_norm(query.reshape(tok_count, query_heads, head_dim), q_gain), query_pos
    ).astype(jnp.bfloat16)
    queries = queries.reshape(tok_count, kv_local, group, head_dim).transpose(1, 2, 0, 3)
    span_keys = rotate(
        rms_norm(key_proj.reshape(tok_count, kv_local, head_dim), k_gain), query_pos
    ).astype(jnp.bfloat16)
    all_keys = jnp.concatenate(
        [ctx_key[0], span_keys.reshape(tok_count, kv_local * head_dim)], axis=0
    )
    all_values = jnp.concatenate([ctx_value[0], value_proj], axis=0)
    key_req = jnp.concatenate([ctx_req, query_req], axis=0)
    key_pos = jnp.concatenate([ctx_pos, query_pos], axis=0)
    scale = 1.0 / math.sqrt(head_dim)
    start_state = (
        jnp.full((kv_local, group, tok_count), -1e30, jnp.float32),
        jnp.zeros((kv_local, group, tok_count), jnp.float32),
        jnp.zeros((kv_local, group, tok_count, head_dim), jnp.float32),
    )
    state = start_state
    piece_keys = lax.all_gather(all_keys, "seq", axis=0, tiled=True)
    piece_values = lax.all_gather(all_values, "seq", axis=0, tiled=True)
    piece_req = lax.all_gather(key_req, "seq", axis=0, tiled=True)
    piece_pos = lax.all_gather(key_pos, "seq", axis=0, tiled=True)
    length = piece_keys.shape[0]
    block = length
    for candidate in (2048, 1280, 1024, 640, 512):
        if length > candidate and length % candidate == 0:
            block = candidate
            break
    count = length // block

    def advance(running, items):
        block_keys, block_values, block_req, block_pos = items
        key_heads = block_keys.reshape(block, kv_local, head_dim)
        value_heads = block_values.reshape(block, kv_local, head_dim)
        visible = (query_req[:, None] == block_req[None, :]) & (
            block_pos[None, :] <= query_pos[:, None]
        )
        largest, total, accum = running
        scores = (
            jnp.einsum("hgtd,khd->hgtk", queries, key_heads, preferred_element_type=jnp.float32)
            * scale
        )
        scores = jnp.where(visible[None, None], scores, -jnp.inf)
        new_largest = jnp.maximum(largest, jnp.max(scores, axis=-1))
        expo = jnp.exp(scores - new_largest[..., None])
        factor = jnp.exp(largest - new_largest)
        total = factor * total + jnp.sum(expo, axis=-1)
        accum = factor[..., None] * accum + jnp.einsum(
            "hgtk,khd->hgtd",
            expo.astype(jnp.bfloat16),
            value_heads,
            preferred_element_type=jnp.float32,
        )
        running = (new_largest, total, accum)
        return (running, None)

    stacked = (
        piece_keys.reshape(count, block, -1),
        piece_values.reshape(count, block, -1),
        piece_req.reshape(count, block),
        piece_pos.reshape(count, block),
    )
    state, _ = lax.scan(advance, state, stacked)
    largest, total, accum = state
    attn = (
        (accum / total[..., None])
        .transpose(2, 0, 1, 3)
        .reshape(tok_count, query_heads * head_dim)
        .astype(jnp.bfloat16)
    )
    half = tok_count // lax.axis_size("tp")
    proj = lax.psum_scatter(
        jnp.dot(attn, w_out, preferred_element_type=jnp.float32).astype(jnp.bfloat16),
        "tp",
        scatter_dimension=0,
        tiled=True,
    ).astype(jnp.float32)
    own_rows = lax.dynamic_slice_in_dim(tokens, lax.axis_index("tp") * half, half, 0)
    resid = (own_rows.astype(jnp.float32) + proj).astype(jnp.bfloat16)
    mixed = rms_norm(resid.astype(jnp.float32), post_gain).astype(jnp.bfloat16)
    top = route_ids.shape[2]
    row_ids = route_ids[0].reshape(-1)
    row_count = row_ids.shape[0]
    seq_tp = lax.axis_size("seq") * lax.axis_size("tp")
    pd_count = lax.axis_size("pd")
    device_count = seq_tp * pd_count
    exp_local = w_gate_up.shape[0]
    experts = device_count * exp_local
    capacity = max(2, 3 * tok_count * top // (2 * lax.axis_size("tp") * experts))
    picks = (row_ids[:, None] == jnp.arange(experts, dtype=jnp.int32)[None, :]).astype(jnp.bfloat16)
    earlier = (
        lax.broadcasted_iota(jnp.int32, (row_count, row_count), 0)
        > lax.broadcasted_iota(jnp.int32, (row_count, row_count), 1)
    ).astype(jnp.bfloat16)
    before = jnp.dot(earlier, picks, preferred_element_type=jnp.float32)
    rank = jnp.sum(before * picks.astype(jnp.float32), axis=1).astype(jnp.int32)
    target = row_ids * capacity + rank
    row_token = jnp.arange(row_count, dtype=jnp.int32) // top
    outgoing = jnp.zeros((experts * capacity, width), jnp.bfloat16).at[target].set(mixed[row_token])
    outgoing = outgoing.reshape(device_count, exp_local, capacity, width)
    returned = lax.all_to_all(
        expert_mlp(
            lax.all_to_all(outgoing, ("seq", "tp", "pd"), split_axis=0, concat_axis=0, tiled=True),
            w_gate_up,
            w_down,
        ),
        ("seq", "tp", "pd"),
        split_axis=0,
        concat_axis=0,
        tiled=True,
    )
    gathered = returned.reshape(experts * capacity, width)[target]
    weights = route_weights[0]
    weights = weights / jnp.sum(weights, axis=-1, keepdims=True)
    moe = jnp.einsum(
        "tkd,tk->td",
        gathered.reshape(half, top, width),
        weights,
        preferred_element_type=jnp.float32,
    )
    layer_out = (resid.astype(jnp.float32) + moe).astype(jnp.bfloat16)[None]
    layers = earlier_kv.shape[0]
    per_device = tok_count // PAGE
    page_count = layers * per_device
    seq_size = lax.axis_size("seq")
    page_cap = max(1, page_count // seq_size)
    pages = earlier_kv[:, 0].reshape(layers, per_device, PAGE, kv_local, 2 * head_dim)
    pages = pages.transpose(3, 0, 1, 2, 4).reshape(kv_local, page_count, PAGE, 2 * head_dim)
    table = page_table[:, 0].transpose(2, 0, 1).reshape(kv_local, page_count)
    owners = table // page_count
    slots = table % page_count
    order = jnp.arange(page_count, dtype=jnp.int32)
    same = (owners[:, :, None] == owners[:, None, :]) & (
        order[None, None, :] < order[None, :, None]
    )
    page_rank = jnp.sum(same.astype(jnp.int32), axis=2)
    page_target = owners * page_cap + page_rank
    head_rows = jnp.broadcast_to(jnp.arange(kv_local, dtype=jnp.int32)[:, None], page_target.shape)
    outgoing_pages = (
        jnp.zeros((kv_local, seq_size * page_cap, PAGE, 2 * head_dim), jnp.bfloat16)
        .at[head_rows, page_target]
        .set(pages)
    )
    outgoing_slots = (
        jnp.full((kv_local, seq_size * page_cap), -1, jnp.int32)
        .at[head_rows, page_target]
        .set(slots)
    )
    arrived_pages, arrived_slots = (
        lax.all_to_all(outgoing_pages, "seq", split_axis=1, concat_axis=1, tiled=True),
        lax.all_to_all(outgoing_slots, "seq", split_axis=1, concat_axis=1, tiled=True),
    )
    placing = (arrived_slots[:, None, :] == order[None, :, None]).astype(jnp.bfloat16)
    cache = jnp.einsum(
        "hkr,hrpc->hkpc", placing, arrived_pages, preferred_element_type=jnp.float32
    ).astype(jnp.bfloat16)
    decode_cache = cache[None, :, None]
    return (layer_out, decode_cache)


def shards_small(
    hidden_in,
    input_gain,
    w_query,
    w_key,
    w_value,
    q_gain,
    k_gain,
    w_out,
    post_gain,
    ctx_key,
    ctx_value,
    span_lens,
    ctx_lens,
    route_ids,
    route_weights,
    w_gate_up,
    w_down,
    earlier_kv,
    page_table,
):
    tokens = hidden_in[0]
    tok_count = tokens.shape[0]
    width = tokens.shape[1]
    ctx_count = ctx_key.shape[1]
    head_dim = q_gain.shape[0]
    seq_index = lax.axis_index("seq")
    span_places = seq_index * tok_count + jnp.arange(tok_count, dtype=jnp.int32)
    query_req, query_pos = query_places(span_lens[0], ctx_lens[0], span_places)
    normed = rms_norm(tokens.astype(jnp.float32), input_gain).astype(jnp.bfloat16)
    query = jnp.dot(normed, w_query, preferred_element_type=jnp.float32)
    key_proj = jnp.dot(normed, w_key, preferred_element_type=jnp.float32)
    value_proj = jnp.dot(normed, w_value, preferred_element_type=jnp.float32).astype(jnp.bfloat16)
    query_heads = w_query.shape[1] // head_dim
    kv_local = w_key.shape[1] // head_dim
    group = query_heads // kv_local
    queries = rotate(
        rms_norm(query.reshape(tok_count, query_heads, head_dim), q_gain), query_pos
    ).astype(jnp.bfloat16)
    queries = queries.reshape(tok_count, kv_local, group, head_dim).transpose(1, 2, 0, 3)
    span_keys = rotate(
        rms_norm(key_proj.reshape(tok_count, kv_local, head_dim), k_gain), query_pos
    ).astype(jnp.bfloat16)
    all_keys = jnp.concatenate(
        [ctx_key[0], span_keys.reshape(tok_count, kv_local * head_dim)], axis=0
    )
    all_values = jnp.concatenate([ctx_value[0], value_proj], axis=0)
    scale = 1.0 / math.sqrt(head_dim)
    start_state = (
        jnp.full((kv_local, group, tok_count), -1e30, jnp.float32),
        jnp.zeros((kv_local, group, tok_count), jnp.float32),
        jnp.zeros((kv_local, group, tok_count, head_dim), jnp.float32),
    )
    state = start_state
    both = gather(jnp.concatenate([all_keys, all_values], axis=1), False, 1)
    both = both.reshape(-1, 2 * head_dim)
    piece_keys, piece_values = both[:, :head_dim], both[:, head_dim:]
    everywhere = jnp.arange(tok_count * lax.axis_size("seq"), dtype=jnp.int32)
    places_req, places_pos = query_places(span_lens[0], ctx_lens[0], everywhere)
    all_ctx = jnp.arange(ctx_count * lax.axis_size("seq"), dtype=jnp.int32)
    prior_req, prior_pos = context_places(ctx_lens[0], all_ctx)
    shape_ctx, shape_tok = (-1, ctx_count), (-1, tok_count)
    piece_req = jnp.concatenate(
        [prior_req.reshape(shape_ctx), places_req.reshape(shape_tok)], axis=1
    ).reshape(-1)
    piece_pos = jnp.concatenate(
        [prior_pos.reshape(shape_ctx), places_pos.reshape(shape_tok)], axis=1
    ).reshape(-1)
    length = piece_keys.shape[0]
    block = length
    for candidate in (2048, 1280, 1024, 640, 512):
        if length > candidate and length % candidate == 0:
            block = candidate
            break
    count = length // block

    def advance(running, items):
        block_keys, block_values, block_req, block_pos = items
        key_heads = block_keys.reshape(block, kv_local, head_dim)
        value_heads = block_values.reshape(block, kv_local, head_dim)
        visible = (query_req[:, None] == block_req[None, :]) & (
            block_pos[None, :] <= query_pos[:, None]
        )
        largest, total, accum = running
        scores = (
            jnp.einsum("hgtd,khd->hgtk", queries, key_heads, preferred_element_type=jnp.float32)
            * scale
        )
        scores = jnp.where(visible[None, None], scores, -jnp.inf)
        new_largest = jnp.maximum(largest, jnp.max(scores, axis=-1))
        expo = jnp.exp(scores - new_largest[..., None])
        factor = jnp.exp(largest - new_largest)
        total = factor * total + jnp.sum(expo, axis=-1)
        accum = factor[..., None] * accum + jnp.einsum(
            "hgtk,khd->hgtd",
            expo.astype(jnp.bfloat16),
            value_heads,
            preferred_element_type=jnp.float32,
        )
        running = (new_largest, total, accum)
        return (running, None)

    stacked = (
        piece_keys.reshape(count, block, -1),
        piece_values.reshape(count, block, -1),
        piece_req.reshape(count, block),
        piece_pos.reshape(count, block),
    )
    state, _ = lax.scan(advance, state, stacked)
    largest, total, accum = state
    attn = (
        (accum / total[..., None])
        .transpose(2, 0, 1, 3)
        .reshape(tok_count, query_heads * head_dim)
        .astype(jnp.bfloat16)
    )
    half = tok_count // lax.axis_size("tp")
    tp_index = lax.axis_index("tp")
    own_attn = lax.dynamic_slice_in_dim(attn, tp_index * half, half, 0)
    other_attn = lax.dynamic_slice_in_dim(attn, (1 - tp_index) * half, half, 0)
    sent = jnp.dot(other_attn, w_out, preferred_element_type=jnp.float32).astype(jnp.bfloat16)
    proj = jnp.dot(own_attn, w_out, preferred_element_type=jnp.float32)
    proj = proj + lax.ppermute(sent, "tp", [(0, 1), (1, 0)]).astype(jnp.float32)
    own_rows = lax.dynamic_slice_in_dim(tokens, lax.axis_index("tp") * half, half, 0)
    resid = (own_rows.astype(jnp.float32) + proj).astype(jnp.bfloat16)
    mixed = rms_norm(resid.astype(jnp.float32), post_gain).astype(jnp.bfloat16)
    top = route_ids.shape[2]
    weights = route_weights[0]
    weights = weights / jnp.sum(weights, axis=-1, keepdims=True)
    high = weights.astype(jnp.bfloat16)
    low = (weights - high.astype(jnp.float32)).astype(jnp.bfloat16)
    notes = jnp.concatenate(
        [
            route_ids[0].astype(jnp.bfloat16),
            high,
            low,
            jnp.zeros((half, 128 - 3 * top), jnp.bfloat16),
        ],
        axis=1,
    )
    gathered = gather(jnp.concatenate([mixed, notes], axis=1), True, 2)
    sources = gathered.reshape(-1, half, width + 128)
    source_count = sources.shape[0]
    capacity = 3 * half * top // 64
    expert = (seq_index * 2 + tp_index) * 2 + lax.axis_index("pd")
    notes = sources[:, :, width:].astype(jnp.float32)
    mine = notes[:, :, :top] == expert.astype(jnp.float32)
    share = jnp.sum(
        jnp.where(mine, notes[:, :, top : 2 * top] + notes[:, :, 2 * top : 3 * top], 0.0), axis=2
    )
    member = jnp.any(mine, axis=2)
    earlier = (
        lax.broadcasted_iota(jnp.int32, (half, half), 0)
        < lax.broadcasted_iota(jnp.int32, (half, half), 1)
    ).astype(jnp.bfloat16)
    rank = jnp.dot(
        member.astype(jnp.bfloat16), earlier, preferred_element_type=jnp.float32
    ).astype(jnp.int32)
    seat = jnp.where(member, rank, -1)
    places = lax.broadcasted_iota(jnp.int32, (source_count, capacity, half), 1)
    chosen = (seat[:, None, :] == places).astype(jnp.bfloat16)
    rows = jnp.einsum(
        "sct,std->scd", chosen, sources[:, :, :width], preferred_element_type=jnp.float32
    ).astype(jnp.bfloat16)
    made = expert_mlp(rows[:, None], w_gate_up, w_down)[:, 0]
    partial = jnp.einsum("sct,scd->std", chosen, made, preferred_element_type=jnp.float32)
    partial = (partial * share[:, :, None]).astype(jnp.bfloat16)
    layer_out = combine(partial.reshape(DEPTH, 2, 2, 2, half, width), resid, 3)
    layer_out = layer_out.astype(jnp.bfloat16)[None]
    layers = earlier_kv.shape[0]
    per_device = tok_count // PAGE
    page_count = layers * per_device
    seq_size = lax.axis_size("seq")
    page_cap = max(1, page_count // seq_size)
    pages = earlier_kv[:, 0].reshape(layers, per_device, PAGE, kv_local, 2 * head_dim)
    pages = pages.transpose(3, 0, 1, 2, 4).reshape(kv_local, page_count, PAGE, 2 * head_dim)
    table = page_table[:, 0].transpose(2, 0, 1).reshape(kv_local, page_count)
    owners = table // page_count
    slots = table % page_count
    order = jnp.arange(page_count, dtype=jnp.int32)
    same = (owners[:, :, None] == owners[:, None, :]) & (
        order[None, None, :] < order[None, :, None]
    )
    page_rank = jnp.sum(same.astype(jnp.int32), axis=2)
    page_target = owners * page_cap + page_rank
    head_rows = jnp.broadcast_to(jnp.arange(kv_local, dtype=jnp.int32)[:, None], page_target.shape)
    outgoing_pages = (
        jnp.zeros((kv_local, seq_size * page_cap, PAGE, 2 * head_dim), jnp.bfloat16)
        .at[head_rows, page_target]
        .set(pages)
    )
    outgoing_slots = (
        jnp.full((kv_local, seq_size * page_cap), -1, jnp.int32)
        .at[head_rows, page_target]
        .set(slots)
    )
    arrived_pages, arrived_slots = (
        lax.all_to_all(outgoing_pages, "seq", split_axis=1, concat_axis=1, tiled=True),
        lax.all_to_all(outgoing_slots, "seq", split_axis=1, concat_axis=1, tiled=True),
    )
    placing = (arrived_slots[:, None, :] == order[None, :, None]).astype(jnp.bfloat16)
    cache = jnp.einsum(
        "hkr,hrpc->hkpc", placing, arrived_pages, preferred_element_type=jnp.float32
    ).astype(jnp.bfloat16)
    decode_cache = cache[None, :, None]
    return (layer_out, decode_cache)


def solution(mesh):
    in_specs = (
        P("pd", "seq", None),
        P(),
        P(None, "tp"),
        P(None, "tp"),
        P(None, "tp"),
        P(),
        P(),
        P("tp", None),
        P(),
        P("pd", "seq", "tp"),
        P("pd", "seq", "tp"),
        P("pd", None),
        P("pd", None),
        P("pd", ("seq", "tp"), None),
        P("pd", ("seq", "tp"), None),
        P(("seq", "tp", "pd"), None, None),
        P(("seq", "tp", "pd"), None, None),
        P(None, "pd", "seq", "tp", None),
        P(None, "pd", "seq", "tp"),
    )
    out_specs = (P("pd", ("seq", "tp"), None), P("seq", "tp", "pd", None, None, None))
    small = mesh.shape["seq"] == 2 * DEPTH and mesh.shape["tp"] == 2 and mesh.shape["pd"] == 2
    per_device = shards_small if small else shards
    return jax.shard_map(per_device, mesh=mesh, in_specs=in_specs, out_specs=out_specs, check_vma=False)
```

```python
import functools
import math

import jax
import jax.numpy as jnp
from jax import lax
from jax.experimental import pallas as pl
from jax.experimental.pallas import tpu as pltpu
from jax.sharding import PartitionSpec as P

PAGE = 128
MESH = pl.DeviceIdType.MESH
DEPTH = 4


def remote(src, dst, send, recv, device):
    return pltpu.make_async_remote_copy(
        src_ref=src,
        dst_ref=dst,
        send_sem=send,
        recv_sem=recv,
        device_id=device,
        device_id_type=MESH,
    )


def position():
    seq = lax.axis_index("seq")
    return seq, seq // 2, seq % 2, lax.axis_index("pd"), lax.axis_index("tp")


def greet(full):
    seq, mz, mx, my, mc = position()
    barrier = pltpu.get_barrier_semaphore()

    @pl.when(mz > 0)
    def _():
        pl.semaphore_signal(barrier, inc=1, device_id={"seq": seq - 2}, device_id_type=MESH)

    @pl.when(mz < DEPTH - 1)
    def _():
        pl.semaphore_signal(barrier, inc=1, device_id={"seq": seq + 2}, device_id_type=MESH)

    others = [{"seq": mz * 2 + 1 - mx}]
    if full:
        others += [{"pd": 1 - my}, {"tp": 1 - mc}]
    for other in others:
        pl.semaphore_signal(barrier, inc=1, device_id=other, device_id_type=MESH)
    ends = (mz > 0).astype(jnp.int32) + (mz < DEPTH - 1).astype(jnp.int32)
    pl.semaphore_wait(barrier, len(others) + ends)


def gather_kernel(full, in_ref, out_ref, lsem, zu, zd, zr, xs, xr, ys, yr, es, er, fs, fr, cs, cr):
    seq, mz, mx, my, mc = position()
    half = in_ref.shape[0] // 2
    xdev, ydev, cdev = {"seq": mz * 2 + 1 - mx}, {"pd": 1 - my}, {"tp": 1 - mc}

    def slot(o, x, y):
        return out_ref.at[o, x, y, mc] if full else out_ref.at[o, x]

    def core_slot(o, x, y, c):
        return out_ref.at[o, x, y, c]

    first, second = pl.ds(0, half), pl.ds(half, half)
    own = pltpu.make_async_copy(in_ref, slot(mz, mx, my), lsem)

    def zup(src, o):
        return remote(src, slot(o, mx, my), zu.at[o], zr.at[o], {"seq": seq + 2})

    def zdown(src, o):
        return remote(src, slot(o, mx, my), zd.at[o], zr.at[o], {"seq": seq - 2})

    def xcopy(src, o, x):
        return remote(src, slot(o, x, my), xs.at[o], xr.at[o], xdev)

    def ycopy(src, o, y):
        return remote(src, slot(o, mx, y), ys.at[o], yr.at[o], ydev)

    def ecopy(o, x, y):
        part = slot(o, x, y).at[first]
        return remote(part, part, es.at[o], er.at[o], ydev)

    def fcopy(o, x, y):
        part = slot(o, x, y).at[second]
        return remote(part, part, fs.at[o], fr.at[o], xdev)

    def ccopy(src, o, x, y, c):
        k = o * 4 + x * 2 + y
        return remote(src, core_slot(o, x, y, c), cs.at[k], cr.at[k], cdev)

    def have_z(o, src, up, down):
        if up:

            @pl.when(mz < DEPTH - 1)
            def _():
                zup(src, o).start()

        if down:

            @pl.when(mz > 0)
            def _():
                zdown(src, o).start()

        xcopy(src, o, mx).start()
        if full:
            ycopy(src, o, my).start()
            ccopy(src, o, mx, my, mc).start()

    def have_xy(o):
        xcopy(slot(o, 1 - mx, my), o, 1 - mx).wait_recv()
        if full:
            ecopy(o, 1 - mx, my).start()
            ccopy(slot(o, 1 - mx, my), o, 1 - mx, my, mc).start()
            ycopy(slot(o, mx, 1 - my), o, 1 - my).wait_recv()
            fcopy(o, mx, 1 - my).start()
            ccopy(slot(o, mx, 1 - my), o, mx, 1 - my, mc).start()

    def have_diagonal(o):
        if full:
            ecopy(o, 1 - mx, 1 - my).wait_recv()
            fcopy(o, 1 - mx, 1 - my).wait_recv()
            ccopy(slot(o, 1 - mx, 1 - my), o, 1 - mx, 1 - my, mc).start()

    def each(step, action):
        if step == 0:
            action(mz)
        elif step > 0:
            pl.when(mz - step >= 0)(lambda: action(mz - step))
            pl.when(mz + step < DEPTH)(lambda: action(mz + step))

    greet(full)
    have_z(mz, in_ref, True, True)
    own.start()
    for step in range(1, DEPTH):

        @pl.when(mz - step >= 0)
        def _():
            o = mz - step
            zup(slot(o, mx, my), o).wait_recv()
            have_z(o, slot(o, mx, my), True, False)

        @pl.when(mz + step < DEPTH)
        def _():
            o = mz + step
            zup(slot(o, mx, my), o).wait_recv()
            have_z(o, slot(o, mx, my), False, True)

        each(step - 1, have_xy)
        each(step - 2, have_diagonal)
    each(DEPTH - 1, have_xy)
    each(DEPTH - 2, have_diagonal)
    each(DEPTH - 1, have_diagonal)
    for o in range(DEPTH):
        block = slot(o, mx, my)
        pl.when((mz < DEPTH - 1) & (mz >= o))(lambda: zup(block, o).wait_send())
        pl.when((mz > 0) & (mz <= o))(lambda: zdown(block, o).wait_send())
        xcopy(block, o, mx).wait_send()
        if full:
            ycopy(block, o, my).wait_send()
            ecopy(o, 1 - mx, my).wait_send()
            fcopy(o, mx, 1 - my).wait_send()
            for x in range(2):
                for y in range(2):
                    done = ccopy(slot(o, x, y), o, x, y, 1 - mc)
                    done.wait_recv()
                    done.wait_send()
    own.wait()


def gather(block, full, collective_id):
    shape = (DEPTH, 2, 2, 2) if full else (DEPTH, 2)
    dma = pltpu.SemaphoreType.DMA
    return pl.pallas_call(
        functools.partial(gather_kernel, full),
        out_shape=jax.ShapeDtypeStruct(shape + block.shape, block.dtype),
        in_specs=[pl.BlockSpec(memory_space=pl.ANY)],
        out_specs=pl.BlockSpec(memory_space=pl.ANY),
        scratch_shapes=[dma] + [dma((DEPTH,))] * 11 + [dma((4 * DEPTH,))] * 2,
        compiler_params=pltpu.CompilerParams(collective_id=collective_id, has_side_effects=True),
        name="gather_full" if full else "gather_seq",
    )(block)


def combine_kernel(
    part_ref, resid_ref, out_ref, s, cb, dx, dy, xb, yb, zub, zdb,
    ls, cs, cr, dxs, dxr, dys, dyr, xs, xr, ys, yr, zs, zur, zdr,
):
    seq, mz, mx, my, mc = position()
    rows = resid_ref.shape[0]
    half = rows // 2
    xdev, ydev, cdev = {"seq": mz * 2 + 1 - mx}, {"pd": 1 - my}, {"tp": 1 - mc}
    first, second = pl.ds(0, half), pl.ds(half, half)
    step_rows = 16
    lower = mz < 2
    far = jnp.where(lower, 3, 0)
    order = [
        far,
        jnp.where(mz == 0, 2, jnp.where(mz == 1, 0, jnp.where(mz == 2, 3, 1))),
        jnp.where((mz == 0) | (mz == 2), 1, 2),
        mz,
    ]
    middle = (mz == 1) | (mz == 2)

    def load(o, x, y):
        return pltpu.make_async_copy(
            part_ref.at[o, x, y, mc], s.at[o, x, y], ls.at[o * 4 + x * 2 + y]
        )

    def core(o, x, y):
        k = o * 4 + x * 2 + y
        return remote(part_ref.at[o, x, y, 1 - mc], cb.at[o, x, y], cs.at[k], cr.at[k], cdev)

    def diag_x(o):
        return remote(s.at[o, 1 - mx, 1 - my].at[first], dx.at[o], dxs.at[o], dxr.at[o], xdev)

    def diag_y(o):
        return remote(s.at[o, 1 - mx, 1 - my].at[second], dy.at[o], dys.at[o], dyr.at[o], ydev)

    def send_x(o):
        return remote(s.at[o, 1 - mx, my], xb.at[o], xs.at[o], xr.at[o], xdev)

    def send_y(o):
        return remote(s.at[o, mx, 1 - my], yb.at[o], ys.at[o], yr.at[o], ydev)

    def send_up(o):
        return remote(s.at[o, mx, my], zub.at[o], zs.at[o], zur.at[o], {"seq": seq + 2})

    def send_down(o):
        return remote(s.at[o, mx, my], zdb.at[o], zs.at[o], zdr.at[o], {"seq": seq - 2})

    def add(target, start, count, *others):
        @pl.loop(0, count // step_rows)
        def _(i):
            at = pl.ds(pl.multiple_of(start + i * step_rows, step_rows), step_rows)
            total = target[at, :].astype(jnp.float32)
            for other in others:
                there = pl.ds(pl.multiple_of(i * step_rows, step_rows), step_rows)
                total = total + other[there, :].astype(jnp.float32)
            target[at, :] = total.astype(target.dtype)

    def begin(o):
        for x, y in ((1 - mx, 1 - my), (1 - mx, my), (mx, 1 - my), (mx, my)):
            core(o, x, y).start()
            load(o, x, y).start()

    def stage_a(o):
        for x, y in ((1 - mx, 1 - my), (1 - mx, my), (mx, 1 - my), (mx, my)):
            load(o, x, y).wait()
            core(o, x, y).wait_recv()
            add(s.at[o, x, y], 0, rows, cb.at[o, x, y])
            if x is not mx and y is not my:
                diag_x(o).start()
                diag_y(o).start()

    def stage_b(o):
        diag_x(o).wait_recv()
        add(s.at[o, mx, 1 - my], 0, half, dx.at[o])
        send_y(o).start()
        diag_y(o).wait_recv()
        add(s.at[o, 1 - mx, my], half, half, dy.at[o])
        send_x(o).start()

    def pass_on(o, incoming):
        up = o > mz

        @pl.when(up)
        def _():
            if incoming:
                send_up(o).wait_recv()
                add(s.at[o, mx, my], 0, rows, zub.at[o])
            send_up(o).start()

        @pl.when(jnp.logical_not(up))
        def _():
            if incoming:
                send_down(o).wait_recv()
                add(s.at[o, mx, my], 0, rows, zdb.at[o])
            send_down(o).start()

    def stage_c(j):
        o = order[j]
        send_x(o).wait_recv()
        send_y(o).wait_recv()
        add(s.at[o, mx, my], 0, rows, xb.at[o], yb.at[o])
        if j < DEPTH - 1:
            pl.when(jnp.logical_not(middle))(lambda: pass_on(o, False))
        for late in {0: (), 1: (0,), 2: (1, 2), 3: ()}[j]:
            pl.when(middle)(lambda: pass_on(order[late], True))

    greet(True)
    for o in order:
        begin(o)
    for t in range(DEPTH + 2):
        if t < DEPTH:
            stage_a(order[t])
        if 1 <= t <= DEPTH:
            stage_b(order[t - 1])
        if t >= 2:
            stage_c(t - 2)

    pl.when(mz > 0)(lambda: send_up(mz).wait_recv())
    pl.when(mz < DEPTH - 1)(lambda: send_down(mz).wait_recv())

    @pl.loop(0, rows // step_rows)
    def _(i):
        at = pl.ds(pl.multiple_of(i * step_rows, step_rows), step_rows)
        out_ref[at, :] = s[mz, mx, my, at, :].astype(jnp.float32) + resid_ref[at, :].astype(
            jnp.float32
        )

    @pl.when(mz > 0)
    def _():
        add(out_ref, 0, rows, zub.at[mz])

    @pl.when(mz < DEPTH - 1)
    def _():
        add(out_ref, 0, rows, zdb.at[mz])

    for o in range(DEPTH):
        for x in range(2):
            for y in range(2):
                core(o, x, y).wait_send()
        diag_x(o).wait_send()
        diag_y(o).wait_send()
        send_x(o).wait_send()
        send_y(o).wait_send()
        pl.when(mz != o)(lambda: send_up(o).wait_send())


def combine(partial, resid, collective_id):
    rows, width = resid.shape
    dma = pltpu.SemaphoreType.DMA
    bf16 = jnp.bfloat16
    vmem = pl.BlockSpec(memory_space=pltpu.VMEM)
    return pl.pallas_call(
        combine_kernel,
        out_shape=jax.ShapeDtypeStruct((rows, width), jnp.float32),
        in_specs=[pl.BlockSpec(memory_space=pl.ANY), vmem],
        out_specs=vmem,
        scratch_shapes=[
            pltpu.VMEM((DEPTH, 2, 2, rows, width), bf16),
            pltpu.VMEM((DEPTH, 2, 2, rows, width), bf16),
            pltpu.VMEM((DEPTH, rows // 2, width), bf16),
            pltpu.VMEM((DEPTH, rows // 2, width), bf16),
        ]
        + [pltpu.VMEM((DEPTH, rows, width), bf16)] * 4
        + [dma((4 * DEPTH,))] * 3
        + [dma((DEPTH,))] * 11,
        compiler_params=pltpu.CompilerParams(
            collective_id=collective_id, has_side_effects=True, vmem_limit_bytes=48 << 20
        ),
        name="combine",
    )(partial, resid)


def rms_norm(values, gain):
    return values * lax.rsqrt(jnp.mean(values * values, axis=-1, keepdims=True) + 1e-06) * gain


def rotate(values, places):
    half = values.shape[-1] // 2
    freq = jnp.exp(
        jnp.arange(half, dtype=jnp.float32) * (-2.0 * math.log(1000000.0) / values.shape[-1])
    )
    angle = places.astype(jnp.float32)[:, None] * freq[None, :]
    cosine = jnp.cos(angle)[:, None, :]
    sine = jnp.sin(angle)[:, None, :]
    first = values[..., :half]
    second = values[..., half:]
    return jnp.concatenate(
        [first * cosine - second * sine, second * cosine + first * sine], axis=-1
    )


def running_sum(counts):
    index = jnp.arange(counts.shape[0], dtype=jnp.int32)
    return jnp.sum(jnp.where(index[None, :] <= index[:, None], counts[None, :], 0), axis=1)


def query_places(lengths, context_lengths, places):
    ends = running_sum(lengths)
    starts = ends - lengths
    request = jnp.sum((places[:, None] >= ends[None, :]).astype(jnp.int32), axis=1)
    member = request[:, None] == jnp.arange(lengths.shape[0], dtype=jnp.int32)[None, :]
    first = jnp.sum(jnp.where(member, starts[None, :], 0), axis=1)
    prior = jnp.sum(jnp.where(member, context_lengths[None, :], 0), axis=1)
    return (request, places - first + prior)


def context_places(context_lengths, places):
    ends = running_sum(context_lengths)
    starts = ends - context_lengths
    request = jnp.sum((places[:, None] >= ends[None, :]).astype(jnp.int32), axis=1)
    member = request[:, None] == jnp.arange(context_lengths.shape[0], dtype=jnp.int32)[None, :]
    first = jnp.sum(jnp.where(member, starts[None, :], 0), axis=1)
    return (request, places - first)


def expert_mlp(arrived, w_gate_up, w_down):
    hidden = jnp.einsum("sejd,edf->sejf", arrived, w_gate_up, preferred_element_type=jnp.float32)
    inner = hidden.shape[-1] // 2
    act = (jax.nn.silu(hidden[..., :inner]) * hidden[..., inner:]).astype(jnp.bfloat16)
    return jnp.einsum("sejf,efd->sejd", act, w_down, preferred_element_type=jnp.float32).astype(
        jnp.bfloat16
    )


def shards(
    hidden_in,
    input_gain,
    w_query,
    w_key,
    w_value,
    q_gain,
    k_gain,
    w_out,
    post_gain,
    ctx_key,
    ctx_value,
    span_lens,
    ctx_lens,
    route_ids,
    route_weights,
    w_gate_up,
    w_down,
    earlier_kv,
    page_table,
):
    tokens = hidden_in[0]
    tok_count = tokens.shape[0]
    width = tokens.shape[1]
    ctx_count = ctx_key.shape[1]
    head_dim = q_gain.shape[0]
    seq_index = lax.axis_index("seq")
    span_places = seq_index * tok_count + jnp.arange(tok_count, dtype=jnp.int32)
    ctx_index = seq_index * ctx_count + jnp.arange(ctx_count, dtype=jnp.int32)
    query_req, query_pos = query_places(span_lens[0], ctx_lens[0], span_places)
    ctx_req, ctx_pos = context_places(ctx_lens[0], ctx_index)
    normed = rms_norm(tokens.astype(jnp.float32), input_gain).astype(jnp.bfloat16)
    query = jnp.dot(normed, w_query, preferred_element_type=jnp.float32)
    key_proj = jnp.dot(normed, w_key, preferred_element_type=jnp.float32)
    value_proj = jnp.dot(normed, w_value, preferred_element_type=jnp.float32).astype(jnp.bfloat16)
    query_heads = w_query.shape[1] // head_dim
    kv_local = w_key.shape[1] // head_dim
    group = query_heads // kv_local
    queries = rotate(
        rms_norm(query.reshape(tok_count, query_heads, head_dim), q_gain), query_pos
    ).astype(jnp.bfloat16)
    queries = queries.reshape(tok_count, kv_local, group, head_dim).transpose(1, 2, 0, 3)
    span_keys = rotate(
        rms_norm(key_proj.reshape(tok_count, kv_local, head_dim), k_gain), query_pos
    ).astype(jnp.bfloat16)
    all_keys = jnp.concatenate(
        [ctx_key[0], span_keys.reshape(tok_count, kv_local * head_dim)], axis=0
    )
    all_values = jnp.concatenate([ctx_value[0], value_proj], axis=0)
    key_req = jnp.concatenate([ctx_req, query_req], axis=0)
    key_pos = jnp.concatenate([ctx_pos, query_pos], axis=0)
    scale = 1.0 / math.sqrt(head_dim)
    start_state = (
        jnp.full((kv_local, group, tok_count), -1e30, jnp.float32),
        jnp.zeros((kv_local, group, tok_count), jnp.float32),
        jnp.zeros((kv_local, group, tok_count, head_dim), jnp.float32),
    )
    state = start_state
    piece_keys = lax.all_gather(all_keys, "seq", axis=0, tiled=True)
    piece_values = lax.all_gather(all_values, "seq", axis=0, tiled=True)
    piece_req = lax.all_gather(key_req, "seq", axis=0, tiled=True)
    piece_pos = lax.all_gather(key_pos, "seq", axis=0, tiled=True)
    length = piece_keys.shape[0]
    block = length
    for candidate in (2048, 1280, 1024, 640, 512):
        if length > candidate and length % candidate == 0:
            block = candidate
            break
    count = length // block

    def advance(running, items):
        block_keys, block_values, block_req, block_pos = items
        key_heads = block_keys.reshape(block, kv_local, head_dim)
        value_heads = block_values.reshape(block, kv_local, head_dim)
        visible = (query_req[:, None] == block_req[None, :]) & (
            block_pos[None, :] <= query_pos[:, None]
        )
        largest, total, accum = running
        scores = (
            jnp.einsum("hgtd,khd->hgtk", queries, key_heads, preferred_element_type=jnp.float32)
            * scale
        )
        scores = jnp.where(visible[None, None], scores, -jnp.inf)
        new_largest = jnp.maximum(largest, jnp.max(scores, axis=-1))
        expo = jnp.exp(scores - new_largest[..., None])
        factor = jnp.exp(largest - new_largest)
        total = factor * total + jnp.sum(expo, axis=-1)
        accum = factor[..., None] * accum + jnp.einsum(
            "hgtk,khd->hgtd",
            expo.astype(jnp.bfloat16),
            value_heads,
            preferred_element_type=jnp.float32,
        )
        running = (new_largest, total, accum)
        return (running, None)

    stacked = (
        piece_keys.reshape(count, block, -1),
        piece_values.reshape(count, block, -1),
        piece_req.reshape(count, block),
        piece_pos.reshape(count, block),
    )
    state, _ = lax.scan(advance, state, stacked)
    largest, total, accum = state
    attn = (
        (accum / total[..., None])
        .transpose(2, 0, 1, 3)
        .reshape(tok_count, query_heads * head_dim)
        .astype(jnp.bfloat16)
    )
    half = tok_count // lax.axis_size("tp")
    proj = lax.psum_scatter(
        jnp.dot(attn, w_out, preferred_element_type=jnp.float32).astype(jnp.bfloat16),
        "tp",
        scatter_dimension=0,
        tiled=True,
    ).astype(jnp.float32)
    own_rows = lax.dynamic_slice_in_dim(tokens, lax.axis_index("tp") * half, half, 0)
    resid = (own_rows.astype(jnp.float32) + proj).astype(jnp.bfloat16)
    mixed = rms_norm(resid.astype(jnp.float32), post_gain).astype(jnp.bfloat16)
    top = route_ids.shape[2]
    row_ids = route_ids[0].reshape(-1)
    row_count = row_ids.shape[0]
    seq_tp = lax.axis_size("seq") * lax.axis_size("tp")
    pd_count = lax.axis_size("pd")
    device_count = seq_tp * pd_count
    exp_local = w_gate_up.shape[0]
    experts = device_count * exp_local
    capacity = max(2, 3 * tok_count * top // (2 * lax.axis_size("tp") * experts))
    picks = (row_ids[:, None] == jnp.arange(experts, dtype=jnp.int32)[None, :]).astype(jnp.bfloat16)
    earlier = (
        lax.broadcasted_iota(jnp.int32, (row_count, row_count), 0)
        > lax.broadcasted_iota(jnp.int32, (row_count, row_count), 1)
    ).astype(jnp.bfloat16)
    before = jnp.dot(earlier, picks, preferred_element_type=jnp.float32)
    rank = jnp.sum(before * picks.astype(jnp.float32), axis=1).astype(jnp.int32)
    target = row_ids * capacity + rank
    row_token = jnp.arange(row_count, dtype=jnp.int32) // top
    outgoing = jnp.zeros((experts * capacity, width), jnp.bfloat16).at[target].set(mixed[row_token])
    outgoing = outgoing.reshape(device_count, exp_local, capacity, width)
    returned = lax.all_to_all(
        expert_mlp(
            lax.all_to_all(outgoing, ("seq", "tp", "pd"), split_axis=0, concat_axis=0, tiled=True),
            w_gate_up,
            w_down,
        ),
        ("seq", "tp", "pd"),
        split_axis=0,
        concat_axis=0,
        tiled=True,
    )
    gathered = returned.reshape(experts * capacity, width)[target]
    weights = route_weights[0]
    weights = weights / jnp.sum(weights, axis=-1, keepdims=True)
    moe = jnp.einsum(
        "tkd,tk->td",
        gathered.reshape(half, top, width),
        weights,
        preferred_element_type=jnp.float32,
    )
    layer_out = (resid.astype(jnp.float32) + moe).astype(jnp.bfloat16)[None]
    layers = earlier_kv.shape[0]
    per_device = tok_count // PAGE
    page_count = layers * per_device
    seq_size = lax.axis_size("seq")
    page_cap = max(1, page_count // seq_size)
    pages = earlier_kv[:, 0].reshape(layers, per_device, PAGE, kv_local, 2 * head_dim)
    pages = pages.transpose(3, 0, 1, 2, 4).reshape(kv_local, page_count, PAGE, 2 * head_dim)
    table = page_table[:, 0].transpose(2, 0, 1).reshape(kv_local, page_count)
    owners = table // page_count
    slots = table % page_count
    order = jnp.arange(page_count, dtype=jnp.int32)
    same = (owners[:, :, None] == owners[:, None, :]) & (
        order[None, None, :] < order[None, :, None]
    )
    page_rank = jnp.sum(same.astype(jnp.int32), axis=2)
    page_target = owners * page_cap + page_rank
    head_rows = jnp.broadcast_to(jnp.arange(kv_local, dtype=jnp.int32)[:, None], page_target.shape)
    outgoing_pages = (
        jnp.zeros((kv_local, seq_size * page_cap, PAGE, 2 * head_dim), jnp.bfloat16)
        .at[head_rows, page_target]
        .set(pages)
    )
    outgoing_slots = (
        jnp.full((kv_local, seq_size * page_cap), -1, jnp.int32)
        .at[head_rows, page_target]
        .set(slots)
    )
    arrived_pages, arrived_slots = (
        lax.all_to_all(outgoing_pages, "seq", split_axis=1, concat_axis=1, tiled=True),
        lax.all_to_all(outgoing_slots, "seq", split_axis=1, concat_axis=1, tiled=True),
    )
    placing = (arrived_slots[:, None, :] == order[None, :, None]).astype(jnp.bfloat16)
    cache = jnp.einsum(
        "hkr,hrpc->hkpc", placing, arrived_pages, preferred_element_type=jnp.float32
    ).astype(jnp.bfloat16)
    decode_cache = cache[None, :, None]
    return (layer_out, decode_cache)


def shards_small(
    hidden_in,
    input_gain,
    w_query,
    w_key,
    w_value,
    q_gain,
    k_gain,
    w_out,
    post_gain,
    ctx_key,
    ctx_value,
    span_lens,
    ctx_lens,
    route_ids,
    route_weights,
    w_gate_up,
    w_down,
    earlier_kv,
    page_table,
):
    tokens = hidden_in[0]
    tok_count = tokens.shape[0]
    width = tokens.shape[1]
    ctx_count = ctx_key.shape[1]
    head_dim = q_gain.shape[0]
    seq_index = lax.axis_index("seq")
    span_places = seq_index * tok_count + jnp.arange(tok_count, dtype=jnp.int32)
    query_req, query_pos = query_places(span_lens[0], ctx_lens[0], span_places)
    normed = rms_norm(tokens.astype(jnp.float32), input_gain).astype(jnp.bfloat16)
    query = jnp.dot(normed, w_query, preferred_element_type=jnp.float32)
    key_proj = jnp.dot(normed, w_key, preferred_element_type=jnp.float32)
    value_proj = jnp.dot(normed, w_value, preferred_element_type=jnp.float32).astype(jnp.bfloat16)
    query_heads = w_query.shape[1] // head_dim
    kv_local = w_key.shape[1] // head_dim
    group = query_heads // kv_local
    queries = rotate(
        rms_norm(query.reshape(tok_count, query_heads, head_dim), q_gain), query_pos
    ).astype(jnp.bfloat16)
    queries = queries.reshape(tok_count, kv_local, group, head_dim).transpose(1, 2, 0, 3)
    layers = earlier_kv.shape[0]
    per_device = tok_count // PAGE
    page_count = layers * per_device
    seq_size = lax.axis_size("seq")
    page_cap = max(1, page_count // seq_size)
    pages = earlier_kv[:, 0].reshape(layers, per_device, PAGE, kv_local, 2 * head_dim)
    pages = pages.transpose(3, 0, 1, 2, 4).reshape(kv_local, page_count, PAGE, 2 * head_dim)
    table = page_table[:, 0].transpose(2, 0, 1).reshape(kv_local, page_count)
    owners = table // page_count
    slots = table % page_count
    order = jnp.arange(page_count, dtype=jnp.int32)
    same = (owners[:, :, None] == owners[:, None, :]) & (
        order[None, None, :] < order[None, :, None]
    )
    page_rank = jnp.sum(same.astype(jnp.int32), axis=2)
    page_target = owners * page_cap + page_rank
    head_rows = jnp.broadcast_to(jnp.arange(kv_local, dtype=jnp.int32)[:, None], page_target.shape)
    outgoing_pages = (
        jnp.zeros((kv_local, seq_size * page_cap, PAGE, 2 * head_dim), jnp.bfloat16)
        .at[head_rows, page_target]
        .set(pages)
    )
    outgoing_slots = (
        jnp.full((kv_local, seq_size * page_cap), -1, jnp.int32)
        .at[head_rows, page_target]
        .set(slots)
    )
    queries, outgoing_pages, outgoing_slots = lax.optimization_barrier(
        (queries, outgoing_pages, outgoing_slots)
    )
    arrived_pages, arrived_slots = (
        lax.all_to_all(outgoing_pages, "seq", split_axis=1, concat_axis=1, tiled=True),
        lax.all_to_all(outgoing_slots, "seq", split_axis=1, concat_axis=1, tiled=True),
    )
    span_keys = rotate(
        rms_norm(key_proj.reshape(tok_count, kv_local, head_dim), k_gain), query_pos
    ).astype(jnp.bfloat16)
    all_keys = jnp.concatenate(
        [ctx_key[0], span_keys.reshape(tok_count, kv_local * head_dim)], axis=0
    )
    all_values = jnp.concatenate([ctx_value[0], value_proj], axis=0)
    scale = 1.0 / math.sqrt(head_dim)
    start_state = (
        jnp.full((kv_local, group, tok_count), -1e30, jnp.float32),
        jnp.zeros((kv_local, group, tok_count), jnp.float32),
        jnp.zeros((kv_local, group, tok_count, head_dim), jnp.float32),
    )
    state = start_state
    both = gather(jnp.concatenate([all_keys, all_values], axis=1), False, 1)
    both = both.reshape(-1, 2 * head_dim)
    piece_keys, piece_values = both[:, :head_dim], both[:, head_dim:]
    everywhere = jnp.arange(tok_count * lax.axis_size("seq"), dtype=jnp.int32)
    places_req, places_pos = query_places(span_lens[0], ctx_lens[0], everywhere)
    all_ctx = jnp.arange(ctx_count * lax.axis_size("seq"), dtype=jnp.int32)
    prior_req, prior_pos = context_places(ctx_lens[0], all_ctx)
    shape_ctx, shape_tok = (-1, ctx_count), (-1, tok_count)
    piece_req = jnp.concatenate(
        [prior_req.reshape(shape_ctx), places_req.reshape(shape_tok)], axis=1
    ).reshape(-1)
    piece_pos = jnp.concatenate(
        [prior_pos.reshape(shape_ctx), places_pos.reshape(shape_tok)], axis=1
    ).reshape(-1)
    length = piece_keys.shape[0]
    block = length
    for candidate in (2048, 1280, 1024, 640, 512):
        if length > candidate and length % candidate == 0:
            block = candidate
            break
    count = length // block

    def advance(running, items):
        block_keys, block_values, block_req, block_pos = items
        key_heads = block_keys.reshape(block, kv_local, head_dim)
        value_heads = block_values.reshape(block, kv_local, head_dim)
        visible = (query_req[:, None] == block_req[None, :]) & (
            block_pos[None, :] <= query_pos[:, None]
        )
        largest, total, accum = running
        scores = (
            jnp.einsum("hgtd,khd->hgtk", queries, key_heads, preferred_element_type=jnp.float32)
            * scale
        )
        scores = jnp.where(visible[None, None], scores, -jnp.inf)
        new_largest = jnp.maximum(largest, jnp.max(scores, axis=-1))
        expo = jnp.exp(scores - new_largest[..., None])
        factor = jnp.exp(largest - new_largest)
        total = factor * total + jnp.sum(expo, axis=-1)
        accum = factor[..., None] * accum + jnp.einsum(
            "hgtk,khd->hgtd",
            expo.astype(jnp.bfloat16),
            value_heads,
            preferred_element_type=jnp.float32,
        )
        running = (new_largest, total, accum)
        return (running, None)

    stacked = (
        piece_keys.reshape(count, block, -1),
        piece_values.reshape(count, block, -1),
        piece_req.reshape(count, block),
        piece_pos.reshape(count, block),
    )
    state, _ = lax.scan(advance, state, stacked)
    largest, total, accum = state
    attn = (
        (accum / total[..., None])
        .transpose(2, 0, 1, 3)
        .reshape(tok_count, query_heads * head_dim)
        .astype(jnp.bfloat16)
    )
    half = tok_count // lax.axis_size("tp")
    tp_index = lax.axis_index("tp")
    own_attn = lax.dynamic_slice_in_dim(attn, tp_index * half, half, 0)
    other_attn = lax.dynamic_slice_in_dim(attn, (1 - tp_index) * half, half, 0)
    sent = jnp.dot(other_attn, w_out, preferred_element_type=jnp.float32).astype(jnp.bfloat16)
    proj = jnp.dot(own_attn, w_out, preferred_element_type=jnp.float32)
    proj = proj + lax.ppermute(sent, "tp", [(0, 1), (1, 0)]).astype(jnp.float32)
    proj, arrived_pages, arrived_slots = lax.optimization_barrier(
        (proj, arrived_pages, arrived_slots)
    )
    own_rows = lax.dynamic_slice_in_dim(tokens, lax.axis_index("tp") * half, half, 0)
    resid = (own_rows.astype(jnp.float32) + proj).astype(jnp.bfloat16)
    mixed = rms_norm(resid.astype(jnp.float32), post_gain).astype(jnp.bfloat16)
    top = route_ids.shape[2]
    weights = route_weights[0]
    weights = weights / jnp.sum(weights, axis=-1, keepdims=True)
    high = weights.astype(jnp.bfloat16)
    low = (weights - high.astype(jnp.float32)).astype(jnp.bfloat16)
    notes = jnp.concatenate(
        [
            route_ids[0].astype(jnp.bfloat16),
            high,
            low,
            jnp.zeros((half, 128 - 3 * top), jnp.bfloat16),
        ],
        axis=1,
    )
    gathered = gather(jnp.concatenate([mixed, notes], axis=1), True, 2)
    sources = gathered.reshape(-1, half, width + 128)
    source_count = sources.shape[0]
    capacity = 3 * half * top // 64
    expert = (seq_index * 2 + tp_index) * 2 + lax.axis_index("pd")
    notes = sources[:, :, width:].astype(jnp.float32)
    mine = notes[:, :, :top] == expert.astype(jnp.float32)
    share = jnp.sum(
        jnp.where(mine, notes[:, :, top : 2 * top] + notes[:, :, 2 * top : 3 * top], 0.0), axis=2
    )
    member = jnp.any(mine, axis=2)
    earlier = (
        lax.broadcasted_iota(jnp.int32, (half, half), 0)
        < lax.broadcasted_iota(jnp.int32, (half, half), 1)
    ).astype(jnp.bfloat16)
    rank = jnp.dot(
        member.astype(jnp.bfloat16), earlier, preferred_element_type=jnp.float32
    ).astype(jnp.int32)
    seat = jnp.where(member, rank, -1)
    places = lax.broadcasted_iota(jnp.int32, (source_count, capacity, half), 1)
    chosen = (seat[:, None, :] == places).astype(jnp.bfloat16)
    rows = jnp.einsum(
        "sct,std->scd", chosen, sources[:, :, :width], preferred_element_type=jnp.float32
    ).astype(jnp.bfloat16)
    made = expert_mlp(rows[:, None], w_gate_up, w_down)[:, 0]
    partial = jnp.einsum("sct,scd->std", chosen, made, preferred_element_type=jnp.float32)
    partial = (partial * share[:, :, None]).astype(jnp.bfloat16)
    layer_out = combine(partial.reshape(DEPTH, 2, 2, 2, half, width), resid, 3)
    layer_out = layer_out.astype(jnp.bfloat16)[None]
    placing = (arrived_slots[:, None, :] == order[None, :, None]).astype(jnp.bfloat16)
    cache = jnp.einsum(
        "hkr,hrpc->hkpc", placing, arrived_pages, preferred_element_type=jnp.float32
    ).astype(jnp.bfloat16)
    decode_cache = cache[None, :, None]
    return (layer_out, decode_cache)


def solution(mesh):
    in_specs = (
        P("pd", "seq", None),
        P(),
        P(None, "tp"),
        P(None, "tp"),
        P(None, "tp"),
        P(),
        P(),
        P("tp", None),
        P(),
        P("pd", "seq", "tp"),
        P("pd", "seq", "tp"),
        P("pd", None),
        P("pd", None),
        P("pd", ("seq", "tp"), None),
        P("pd", ("seq", "tp"), None),
        P(("seq", "tp", "pd"), None, None),
        P(("seq", "tp", "pd"), None, None),
        P(None, "pd", "seq", "tp", None),
        P(None, "pd", "seq", "tp"),
    )
    out_specs = (P("pd", ("seq", "tp"), None), P("seq", "tp", "pd", None, None, None))
    small = mesh.shape["seq"] == 2 * DEPTH and mesh.shape["tp"] == 2 and mesh.shape["pd"] == 2
    per_device = shards_small if small else shards
    return jax.shard_map(per_device, mesh=mesh, in_specs=in_specs, out_specs=out_specs, check_vma=False)
```
